32 devices in a mesh: groups: 2 (over x), frame: 16 (over z, y, core).
Axes of the slice: x: 2, y: 2, z: 4, core: 2. Of those that a mesh axis runs over, the one named last changes fastest.
Arguments:
- queries: bfloat16 [4096, 2048], P(('groups', 'frame')), parts along dimension 0, may hold values from -40 to 40, as said below
- key_rows: bfloat16 [4096, 2048], P(('groups', 'frame')), parts along dimension 0, may hold values from -4 to 4
- value_rows: bfloat16 [4096, 2048], P(('groups', 'frame')), parts along dimension 0, may hold values from -6 to 6
- slopes: bfloat16 [16], replicated, may hold values from 0.0019989014 to 0.19921875
- noise_level: int32 [32], P('groups'), parts along dimension 0, may hold values from 0 to 999
- frame_times: int32 [32], P('groups'), parts along dimension 0, may hold values from 0 to 30, as said below
Outputs:
- advanced: bfloat16 [4096, 2048], P(('groups', 'frame')), parts along dimension 0
The draws below stay inside these ranges and needn't reach their ends.
There are 2 independent parts, one for each index of `groups`. The reference program is written for one: setup_inputs(seed, part) draws one part's arguments, and reference() takes and returns one part's arrays. A program takes and returns all parts, laid end to end along the dimension named above; an argument that names none is the same for every part. Nothing has to cross between parts.
Inputs may be any that keep to these rules, and one draw needn't show every extreme that they name: Rows of queries may be large multiples of key rows. `frame_times`: strictly increasing along the window, starting at 0; neighbouring frames differ by 1 to 3; the last frame stands at 30.
All inputs are finite; a program needn't handle non-finite values.
Results may differ from the reference program's by a relative error of at most 0.009.
Values may be sent and summed in bfloat16 or wider, within the bound.
A program may use at most 64 MiB of HBM per device.

```python
import math
import jax
import jax.numpy as jnp
from jax import lax

H = 16
HD = 128
D = 2048
FT = 128
FRAMES = 16
TOKENS = 2048
LEVELS = 1000


def paired_rows(key):
    base = jax.random.fold_in(key, 7)
    query_key, row_key = jax.random.split(base, 2)
    total = FRAMES * FT
    query_vals = jnp.clip(jax.random.normal(query_key, (total, D), jnp.float32), -4.0, 4.0)
    key_vals = jnp.clip(jax.random.normal(row_key, (total, D), jnp.float32), -4.0, 4.0)
    return (query_vals, key_vals)


def draw_queries(key, part):
    return paired_rows(key)[0].astype(jnp.bfloat16)


def draw_key_rows(key, part):
    return paired_rows(key)[1].astype(jnp.bfloat16)


def draw_frame_times(key, part):
    gap_count = FRAMES - 1
    half_count = (FRAMES - 2) // 2
    position = jnp.arange(gap_count, dtype=jnp.int32)
    offsets = jnp.where(position < half_count, -1, jnp.where(position < 2 * half_count, 1, 0)).astype(jnp.int32)
    mixed_offsets = jax.random.permutation(jax.random.fold_in(key, 11), offsets)
    gaps = 2 + mixed_offsets
    stamps = jnp.concatenate([jnp.zeros((1,), jnp.int32), jnp.cumsum(gaps).astype(jnp.int32)])
    return stamps.astype(jnp.int32)


def place_ends(array, own_key, low, high):
    longest = array.shape.index(max(array.shape))
    spots = []
    for shift in (0, 1):
        where = [jax.random.randint(jax.random.fold_in(own_key, axis), (), 0, length) for axis, length in enumerate(array.shape)]
        where[longest] = (where[longest] + shift) % array.shape[longest]
        spots.append(tuple(where))
    return array.at[spots[0]].set(low).at[spots[1]].set(high)


def shard_levels(rng, extent, cuts, least, largest):
    def one(dim, shards_of):
        steps = jax.random.uniform(jax.random.fold_in(jax.random.fold_in(rng, 6), dim), (shards_of,), jnp.float32, least / len(cuts), largest / len(cuts))
        return jnp.repeat(jnp.exp(steps), extent[dim] // shards_of).reshape((-1,) + (1,) * (len(extent) - dim - 1))

    factor_of = one(*cuts[0])
    for cut in cuts[1:]:
        factor_of = factor_of * one(*cut)
    return factor_of


def normal_values(stream_key, extent, width, limit, shards=(), held_as=jnp.bfloat16):
    drawn = width * jax.random.normal(stream_key, extent, jnp.float32)
    if shards:
        drawn = drawn * shard_levels(stream_key, extent, shards, -0.22, 0.18)
    return jnp.clip(drawn, -limit, limit).astype(held_as)


def setup_inputs(seed: int = 0, part: int = 0) -> dict:
    seeds = jax.random.split(jax.random.key(seed), 7)
    part_keys = jax.random.split(jax.random.fold_in(seeds[6], part), 7)
    return {
        "queries": draw_queries(jax.random.fold_in(jax.random.fold_in(seeds[6], part), 71), part),
        "key_rows": draw_key_rows(jax.random.fold_in(jax.random.fold_in(seeds[6], part), 71), part),
        "value_rows": normal_values(part_keys[2], (TOKENS, D), 1.0, 6.0, ((0, 16),)),
        "slopes": jnp.clip(jnp.exp(jax.random.uniform(seeds[3], (H,), jnp.float32, math.log(0.0019989014), math.log(0.19921875))), 0.0019989014, 0.19921875).astype(jnp.bfloat16),
        "noise_level": place_ends(jax.random.randint(part_keys[4], (FRAMES,), 0, LEVELS), jax.random.fold_in(part_keys[4], 1), 0, LEVELS - 1).astype(jnp.int32),
        "frame_times": draw_frame_times(jax.random.fold_in(jax.random.fold_in(seeds[6], part), 71), part),
    }


def noise_gates(noise_level):
    phase = (noise_level.astype(jnp.float32) / LEVELS + 0.008) / 1.008
    cosine = jnp.cos(phase * (math.pi / 2))
    signal = cosine * cosine
    return (jnp.sqrt(signal), jnp.sqrt(1.0 - signal))

def spatial_frame(block):
    query_frame, key_frame, value_frame = block
    query_heads = query_frame.reshape(FT, H, HD).astype(jnp.float32)
    key_heads = key_frame.reshape(FT, H, HD).astype(jnp.float32)
    value_heads = value_frame.reshape(FT, H, HD).astype(jnp.float32)
    scores = jnp.einsum('qhd,khd->hqk', query_heads, key_heads) / math.sqrt(HD)
    weights = jax.nn.softmax(scores, axis=-1).astype(jnp.bfloat16)
    attended = jnp.einsum('hqk,khd->qhd', weights.astype(jnp.float32), value_heads)
    return attended.reshape(FT, H * HD)

def reference(queries, key_rows, value_rows, slopes, noise_level, frame_times):
    signal_gate, noise_gate = noise_gates(noise_level)
    framed = (queries.reshape(FRAMES, FT, D), key_rows.reshape(FRAMES, FT, D), value_rows.reshape(FRAMES, FT, D))
    spatial = lax.map(spatial_frame, framed)
    distance = jnp.abs(frame_times[:, None] - frame_times[None, :]).astype(jnp.float32)
    penalty = -slopes.astype(jnp.float32)[:, None, None] * distance[None]
    blk_size = math.gcd(FT, 64)
    blk_count = FT // blk_size

    def arrange(source):
        return jnp.moveaxis(source.reshape(FRAMES, blk_count, blk_size, H, HD), 1, 0)

    def temporal_block(block):
        query_blk, key_blk, value_blk = block
        scores = jnp.einsum('qbhd,kbhd->bhqk', query_blk.astype(jnp.float32), key_blk.astype(jnp.float32)) / math.sqrt(HD)
        scores = scores + penalty[None]
        weights = jax.nn.softmax(scores, axis=-1).astype(jnp.bfloat16)
        attended = jnp.einsum('bhqk,kbhd->qbhd', weights.astype(jnp.float32), value_blk.astype(jnp.float32))
        return (attended * noise_gate[:, None, None, None]).astype(jnp.bfloat16)
    temporal = lax.map(temporal_block, (arrange(queries), arrange(key_rows), arrange(value_rows)))
    temporal = jnp.moveaxis(temporal, 0, 1).reshape(FRAMES, FT, D)
    mixed = (signal_gate[:, None, None] * spatial + temporal.astype(jnp.float32)).astype(jnp.bfloat16)
    mixed = mixed.reshape(TOKENS, D)
    return jnp.concatenate([mixed[FT:], jnp.zeros((FT, D), jnp.bfloat16)], axis=0)
```

```python
import functools
import math

import jax
import jax.numpy as jnp
from jax import lax
from jax.experimental import pallas as pl
from jax.experimental.pallas import tpu as pltpu
from jax.sharding import PartitionSpec as P

LEVELS = 1000
ROWS = 16
LANES = 128
FAR = 1e30
MESH = pl.DeviceIdType.MESH


def softmax_rows(scores):
    top = jnp.max(scores, axis=-1, keepdims=True)
    raised = jnp.exp(scores - top)
    return (raised * (1.0 / jnp.sum(raised, axis=-1, keepdims=True))).astype(jnp.bfloat16)


def scores_of(queries, keys):
    return lax.dot_general(
        queries, keys, (((1,), (1,)), ((), ())), preferred_element_type=jnp.float32
    )


def kernel(
    n, plan,
    slopes_ref, level_ref, times_ref, q_ref, k_ref, v_ref, out_ref,
    qkv, recv, temporal, ret, sent, carried, dist, signal_gate, noise_gate,
    load_sem, send_sem, recv_sem, back_send_sem, back_recv_sem, carry_send_sem, carry_recv_sem,
):
    frame_rows, width, head_count, head_dim, row_blocks, col_blocks, chunks = plan
    block_cols = width // col_blocks
    cols = block_cols // chunks
    total = n * ROWS
    scale = 1.0 / math.sqrt(head_dim)
    me = lax.axis_index("frame")

    loads = [
        pltpu.make_async_copy(source, qkv.at[i], load_sem.at[i])
        for i, source in enumerate((q_ref, k_ref, v_ref))
    ]
    for load in loads:
        load.start()
    barrier = pltpu.get_barrier_semaphore()

    @pl.loop(1, n)
    def _(step):
        pl.semaphore_signal(
            barrier, inc=1, device_id={"frame": lax.rem(me + step, n)}, device_id_type=MESH
        )

    pl.semaphore_wait(barrier, n - 1)
    for load in loads:
        load.wait()

    def piece(peer, chunk):
        row = pl.multiple_of(lax.div(peer, col_blocks) * ROWS, ROWS)
        col = pl.multiple_of(lax.rem(peer, col_blocks) * block_cols + chunk * cols, LANES)
        return qkv.at[:, pl.ds(row, ROWS), pl.ds(col, cols)]

    my_slot = pl.ds(pl.multiple_of(me * ROWS, ROWS), ROWS)
    my_rows = pl.ds(pl.multiple_of(lax.div(me, col_blocks) * ROWS, ROWS), ROWS)
    my_col = pl.ds(pl.multiple_of(lax.rem(me, col_blocks) * cols, LANES), cols)
    first_head = lax.rem(me, col_blocks) * (block_cols // head_dim)

    @pl.loop(0, chunks)
    def _(chunk):
        @pl.loop(1, n)
        def _(step):
            peer = lax.rem(me + step, n)
            pltpu.make_async_remote_copy(
                src_ref=piece(peer, chunk),
                dst_ref=recv.at[chunk, :, my_slot, :],
                send_sem=send_sem.at[chunk],
                recv_sem=recv_sem.at[chunk],
                device_id={"frame": peer},
                device_id_type=MESH,
            ).start()

        pltpu.make_async_copy(
            piece(me, chunk), recv.at[chunk, :, my_slot, :], recv_sem.at[chunk]
        ).start()

    row_frame = lax.broadcasted_iota(jnp.int32, (n, LANES), 0)

    def place(f, level):
        return jnp.where(row_frame == f, level_ref[f].astype(jnp.float32), level)

    level = lax.fori_loop(0, n, place, jnp.zeros((n, LANES), jnp.float32))
    phase = (level / LEVELS + 0.008) / 1.008
    cosine = jnp.cos(phase * (math.pi / 2))
    signal = cosine * cosine
    signal_gate[...] = jnp.sqrt(signal)
    noise_gate[...] = jnp.sqrt(1.0 - signal)

    own_gate = signal_gate[pl.ds(me, 1), :]

    @pl.loop(0, head_count, unroll=4)
    def _(h):
        at = pl.ds(pl.multiple_of(h * head_dim, LANES), head_dim)
        weights = softmax_rows(scores_of(qkv[0, :, at], qkv[1, :, at]) * scale)
        attended = jnp.dot(weights, qkv[2, :, at], preferred_element_type=jnp.float32)
        sent[:, at] = (attended * own_gate).astype(jnp.bfloat16)

    def carry():
        return pltpu.make_async_remote_copy(
            src_ref=sent,
            dst_ref=carried,
            send_sem=carry_send_sem,
            recv_sem=carry_recv_sem,
            device_id={"frame": lax.rem(me + n - 1, n)},
            device_id_type=MESH,
        )

    @pl.when(me > 0)
    def _():
        carry().start()

    column = lax.broadcasted_iota(jnp.int32, (ROWS, total), 1)
    token = lax.broadcasted_iota(jnp.int32, (ROWS, total), 0)
    same = lax.rem(column, ROWS) == token
    column_frame = lax.div(column, ROWS)

    def stamp(g, stamps):
        return jnp.where(column_frame == g, times_ref[g].astype(jnp.float32), stamps)

    stamps = lax.fori_loop(0, n, stamp, jnp.zeros((ROWS, total), jnp.float32))

    @pl.loop(0, n)
    def _(f):
        gap = jnp.abs(times_ref[f].astype(jnp.float32) - stamps)
        dist[pl.ds(pl.multiple_of(f * ROWS, ROWS), ROWS), :] = jnp.where(same, gap, FAR)

    group = math.gcd(n, 16)

    def temporal_block(chunk, head, start):
        at = pl.ds(head * head_dim, head_dim)
        rows = pl.ds(start * ROWS, group * ROWS) if isinstance(start, int) else pl.ds(
            pl.multiple_of(start * ROWS, ROWS), group * ROWS
        )
        slope = slopes_ref[first_head + chunk * (cols // head_dim) + head]
        raw = scores_of(recv[chunk, 0, rows, at], recv[chunk, 1, :, at])
        weights = softmax_rows(raw * scale - slope * dist[rows, :])
        attended = jnp.dot(weights, recv[chunk, 2, :, at], preferred_element_type=jnp.float32)
        gates = noise_gate[pl.ds(start, group), :]
        gated = attended.reshape(group, ROWS, head_dim) * gates[:, None, :]
        temporal[chunk, rows, at] = gated.reshape(group * ROWS, head_dim).astype(jnp.bfloat16)

    for chunk in range(chunks):
        whole = recv.at[chunk]
        pltpu.make_async_copy(whole, whole, recv_sem.at[chunk]).wait()
        for head in range(cols // head_dim):
            if n == group:
                temporal_block(chunk, head, 0)
            else:
                @pl.loop(0, n // group)
                def _(i):
                    temporal_block(chunk, head, i * group)

        @pl.loop(0, n)
        def _(step):
            peer = lax.rem(me + step, n)

            @pl.when(peer < n - 1)
            def _():
                source = temporal.at[chunk, pl.ds(pl.multiple_of((peer + 1) * ROWS, ROWS), ROWS), :]
                target = ret.at[chunk, my_rows, my_col]

                @pl.when(step > 0)
                def _():
                    pltpu.make_async_remote_copy(
                        src_ref=source,
                        dst_ref=target,
                        send_sem=back_send_sem.at[chunk],
                        recv_sem=back_recv_sem.at[chunk],
                        device_id={"frame": peer},
                        device_id_type=MESH,
                    ).start()

                @pl.when(step == 0)
                def _():
                    pltpu.make_async_copy(source, target, back_recv_sem.at[chunk]).start()

    @pl.when(me < n - 1)
    def _():
        carry().wait_recv()
        for chunk in range(chunks):
            whole = ret.at[chunk]
            pltpu.make_async_copy(whole, whole, back_recv_sem.at[chunk]).wait()
            for block in range(col_blocks):
                at = pl.ds(block * block_cols + chunk * cols, cols)
                out_ref[:, at] = (
                    carried[:, at].astype(jnp.float32)
                    + ret[chunk, :, block * cols:(block + 1) * cols].astype(jnp.float32)
                ).astype(jnp.bfloat16)

    @pl.when(me == n - 1)
    def _():
        out_ref[...] = jnp.zeros_like(out_ref)

    @pl.when(me > 0)
    def _():
        carry().wait_send()

    for chunk in range(chunks):
        part = recv.at[chunk, :, pl.ds(0, total - ROWS), :]
        pltpu.make_async_copy(part, part, send_sem.at[chunk]).wait()

        @pl.when(me < n - 1)
        def _():
            part = temporal.at[chunk, pl.ds(0, total - 2 * ROWS), :]
            pltpu.make_async_copy(part, part, back_send_sem.at[chunk]).wait()

        @pl.when(me == n - 1)
        def _():
            part = temporal.at[chunk, pl.ds(0, total - ROWS), :]
            pltpu.make_async_copy(part, part, back_send_sem.at[chunk]).wait()


def body(queries, key_rows, value_rows, slopes, noise_level, frame_times):
    n = lax.axis_size("frame")
    frame_rows, width = queries.shape
    head_count = slopes.shape[0]
    head_dim = width // head_count
    row_blocks = frame_rows // ROWS
    col_blocks = n // row_blocks
    block_cols = width // col_blocks
    chunks = math.gcd(block_cols // head_dim, 4)
    cols = block_cols // chunks
    total = n * ROWS
    plan = (frame_rows, width, head_count, head_dim, row_blocks, col_blocks, chunks)
    bf16, f32 = jnp.bfloat16, jnp.float32
    smem = pl.BlockSpec(memory_space=pltpu.SMEM)
    anywhere = pl.BlockSpec(memory_space=pl.ANY)
    return pl.pallas_call(
        functools.partial(kernel, n, plan),
        out_shape=jax.ShapeDtypeStruct((frame_rows, width), bf16),
        in_specs=[smem] * 3 + [anywhere] * 3,
        out_specs=pl.BlockSpec(memory_space=pltpu.VMEM),
        scratch_shapes=[
            pltpu.VMEM((3, frame_rows, width), bf16),
            pltpu.VMEM((chunks, 3, total, cols), bf16),
            pltpu.VMEM((chunks, total, cols), bf16),
            pltpu.VMEM((chunks, frame_rows, col_blocks * cols), bf16),
            pltpu.VMEM((frame_rows, width), bf16),
            pltpu.VMEM((frame_rows, width), bf16),
            pltpu.VMEM((total, total), f32),
            pltpu.VMEM((n, LANES), f32),
            pltpu.VMEM((n, LANES), f32),
            pltpu.SemaphoreType.DMA((3,)),
            pltpu.SemaphoreType.DMA((chunks,)),
            pltpu.SemaphoreType.DMA((chunks,)),
            pltpu.SemaphoreType.DMA((chunks,)),
            pltpu.SemaphoreType.DMA((chunks,)),
            pltpu.SemaphoreType.DMA,
            pltpu.SemaphoreType.DMA,
        ],
        compiler_params=pltpu.CompilerParams(
            collective_id=0, has_side_effects=True, vmem_limit_bytes=48 * 1024 * 1024
        ),
    )(slopes.astype(f32), noise_level, frame_times, queries, key_rows, value_rows)


def solution(mesh):
    return jax.shard_map(
        body,
        mesh=mesh,
        in_specs=(
            P(("groups", "frame"), None),
            P(("groups", "frame"), None),
            P(("groups", "frame"), None),
            P(),
            P("groups"),
            P("groups"),
        ),
        out_specs=P(("groups", "frame"), None),
        check_vma=False,
    )
```

```python
import functools
import math

import jax
import jax.numpy as jnp
from jax import lax
from jax.experimental import pallas as pl
from jax.experimental.pallas import tpu as pltpu
from jax.sharding import PartitionSpec as P

LEVELS = 1000
ROWS = 16
LANES = 128
FAR = 1e30
MESH = pl.DeviceIdType.MESH


def softmax_rows(scores):
    top = jnp.max(scores, axis=-1, keepdims=True)
    raised = jnp.exp(scores - top)
    return (raised * (1.0 / jnp.sum(raised, axis=-1, keepdims=True))).astype(jnp.bfloat16)


def scores_of(queries, keys):
    return lax.dot_general(
        queries, keys, (((1,), (1,)), ((), ())), preferred_element_type=jnp.float32
    )


def kernel(
    n, plan,
    slopes_hbm, level_hbm, times_hbm, q_ref, k_ref, v_ref, out_ref,
    qkv, recv, temporal, ret, sent, carried, middle, mixed, dist, signal_gate, noise_gate,
    slopes_ref, level_ref, times_ref, slope_rows,
    load_sem, send_sem, recv_sem, back_send_sem, back_recv_sem, carry_send_sem, carry_recv_sem,
    middle_send_sem, middle_recv_sem, mixed_send_sem,
):
    frame_rows, width, head_count, head_dim, row_blocks, col_blocks, chunks = plan
    block_cols = width // col_blocks
    cols = block_cols // chunks
    total = n * ROWS
    scale = 1.0 / math.sqrt(head_dim)
    half = n // 2
    me = lax.axis_index("frame")

    loads = [
        pltpu.make_async_copy(source, qkv.at[i], load_sem.at[i])
        for i, source in enumerate((q_ref, k_ref, v_ref))
    ]
    small = [
        pltpu.make_async_copy(source, target, load_sem.at[3 + i])
        for i, (source, target) in enumerate(
            ((slopes_hbm, slopes_ref), (level_hbm, level_ref), (times_hbm, times_ref))
        )
    ]
    barrier = pltpu.get_barrier_semaphore()

    @pl.loop(1, n)
    def _(step):
        pl.semaphore_signal(
            barrier, inc=1, device_id={"frame": lax.rem(me + step, n)}, device_id_type=MESH
        )

    for load in loads + small:
        load.start()
    pl.semaphore_wait(barrier, n - 1)
    for load in loads:
        load.wait()

    def block_at(peer):
        row = pl.multiple_of(lax.div(peer, col_blocks) * ROWS, ROWS)
        col = pl.multiple_of(lax.rem(peer, col_blocks) * block_cols, LANES)
        return pl.ds(row, ROWS), pl.ds(col, block_cols)

    def piece(peer, chunk):
        row = pl.multiple_of(lax.div(peer, col_blocks) * ROWS, ROWS)
        col = pl.multiple_of(lax.rem(peer, col_blocks) * block_cols + chunk * cols, LANES)
        return qkv.at[:, pl.ds(row, ROWS), pl.ds(col, cols)]

    my_slot = pl.ds(pl.multiple_of(me * ROWS, ROWS), ROWS)
    my_rows = pl.ds(pl.multiple_of(lax.div(me, col_blocks) * ROWS, ROWS), ROWS)
    my_col = pl.ds(pl.multiple_of(lax.rem(me, col_blocks) * cols, LANES), cols)
    first_head = lax.rem(me, col_blocks) * (block_cols // head_dim)

    @pl.loop(0, chunks)
    def _(chunk):
        @pl.loop(1, n)
        def _(step):
            peer = lax.rem(me + step, n)
            pltpu.make_async_remote_copy(
                src_ref=piece(peer, chunk),
                dst_ref=recv.at[chunk, :, my_slot, :],
                send_sem=send_sem.at[chunk],
                recv_sem=recv_sem.at[chunk],
                device_id={"frame": peer},
                device_id_type=MESH,
            ).start()

        pltpu.make_async_copy(
            piece(me, chunk), recv.at[chunk, :, my_slot, :], recv_sem.at[chunk]
        ).start()

    for load in small:
        load.wait()
    square = (head_count, head_count)
    diagonal = lax.broadcasted_iota(jnp.int32, square, 0) == lax.broadcasted_iota(jnp.int32, square, 1)
    spread = jnp.broadcast_to(slopes_ref[...].astype(jnp.float32).reshape(1, head_count), square)
    slope_rows[...] = jnp.broadcast_to(
        jnp.sum(jnp.where(diagonal, spread, 0.0), axis=1, keepdims=True), slope_rows.shape
    )

    row_frame = lax.broadcasted_iota(jnp.int32, (n, LANES), 0)

    def place(f, level):
        return jnp.where(row_frame == f, level_ref[f].astype(jnp.float32), level)

    level = lax.fori_loop(0, n, place, jnp.zeros((n, LANES), jnp.float32))
    phase = (level / LEVELS + 0.008) / 1.008
    cosine = jnp.cos(phase * (math.pi / 2))
    signal = cosine * cosine
    signal_gate[...] = jnp.sqrt(signal)
    noise_gate[...] = jnp.sqrt(1.0 - signal)

    own_gate = signal_gate[pl.ds(me, 1), :]

    @pl.loop(0, head_count, unroll=4)
    def _(h):
        at = pl.ds(pl.multiple_of(h * head_dim, LANES), head_dim)
        weights = softmax_rows(scores_of(qkv[0, :, at], qkv[1, :, at]) * scale)
        attended = jnp.dot(weights, qkv[2, :, at], preferred_element_type=jnp.float32)
        sent[:, at] = (attended * own_gate).astype(jnp.bfloat16)

    def carry():
        return pltpu.make_async_remote_copy(
            src_ref=sent,
            dst_ref=carried,
            send_sem=carry_send_sem,
            recv_sem=carry_recv_sem,
            device_id={"frame": lax.rem(me + n - 1, n)},
            device_id_type=MESH,
        )

    carries = (me > 0) & (me != half)

    @pl.when(carries)
    def _():
        carry().start()

    @pl.when(me == half)
    def _():
        @pl.loop(1, n)
        def _(step):
            peer = lax.rem(me + step, n)
            pltpu.make_async_remote_copy(
                src_ref=sent.at[block_at(peer)],
                dst_ref=middle,
                send_sem=middle_send_sem,
                recv_sem=middle_recv_sem,
                device_id={"frame": peer},
                device_id_type=MESH,
            ).start()

        pltpu.make_async_copy(sent.at[block_at(me)], middle, middle_recv_sem).start()

    column = lax.broadcasted_iota(jnp.int32, (ROWS, total), 1)
    token = lax.broadcasted_iota(jnp.int32, (ROWS, total), 0)
    same = lax.rem(column, ROWS) == token
    column_frame = lax.div(column, ROWS)

    def stamp(g, stamps):
        return jnp.where(column_frame == g, times_ref[g].astype(jnp.float32), stamps)

    stamps = lax.fori_loop(0, n, stamp, jnp.zeros((ROWS, total), jnp.float32))

    @pl.loop(0, n)
    def _(f):
        gap = jnp.abs(times_ref[f].astype(jnp.float32) - stamps)
        dist[pl.ds(pl.multiple_of(f * ROWS, ROWS), ROWS), :] = jnp.where(same, gap, FAR)

    group = math.gcd(n, 16)

    def temporal_block(chunk, head, start):
        at = pl.ds(head * head_dim, head_dim)
        rows = pl.ds(start * ROWS, group * ROWS) if isinstance(start, int) else pl.ds(
            pl.multiple_of(start * ROWS, ROWS), group * ROWS
        )
        slope = slope_rows[pl.ds(first_head + chunk * (cols // head_dim) + head, 1), :][:, :1]
        raw = scores_of(recv[chunk, 0, rows, at], recv[chunk, 1, :, at])
        weights = softmax_rows(raw * scale - slope * dist[rows, :])
        attended = jnp.dot(weights, recv[chunk, 2, :, at], preferred_element_type=jnp.float32)
        gates = noise_gate[pl.ds(start, group), :]
        gated = attended.reshape(group, ROWS, head_dim) * gates[:, None, :]
        temporal[chunk, rows, at] = gated.reshape(group * ROWS, head_dim).astype(jnp.bfloat16)

    for chunk in range(chunks):
        whole = recv.at[chunk]
        pltpu.make_async_copy(whole, whole, recv_sem.at[chunk]).wait()
        for head in range(cols // head_dim):
            if n == group:
                temporal_block(chunk, head, 0)
            else:
                @pl.loop(0, n // group)
                def _(i):
                    temporal_block(chunk, head, i * group)

        @pl.loop(0, n)
        def _(step):
            peer = lax.rem(me + step, n)

            @pl.when((peer < n - 1) & (peer != half - 1))
            def _():
                source = temporal.at[chunk, pl.ds(pl.multiple_of((peer + 1) * ROWS, ROWS), ROWS), :]
                target = ret.at[chunk, my_rows, my_col]

                @pl.when(step > 0)
                def _():
                    pltpu.make_async_remote_copy(
                        src_ref=source,
                        dst_ref=target,
                        send_sem=back_send_sem.at[chunk],
                        recv_sem=back_recv_sem.at[chunk],
                        device_id={"frame": peer},
                        device_id_type=MESH,
                    ).start()

                @pl.when(step == 0)
                def _():
                    pltpu.make_async_copy(source, target, back_recv_sem.at[chunk]).start()

    pltpu.make_async_copy(middle, middle, middle_recv_sem).wait()
    for chunk in range(chunks):
        at = pl.ds(chunk * cols, cols)
        mixed[:, at] = (
            temporal[chunk, half * ROWS:(half + 1) * ROWS, :].astype(jnp.float32)
            + middle[:, at].astype(jnp.float32)
        ).astype(jnp.bfloat16)
    last = pltpu.make_async_remote_copy(
        src_ref=mixed,
        dst_ref=carried.at[block_at(me)],
        send_sem=mixed_send_sem,
        recv_sem=carry_recv_sem,
        device_id={"frame": half - 1},
        device_id_type=MESH,
    )

    @pl.when(me != half - 1)
    def _():
        last.start()

    @pl.when(me == half - 1)
    def _():
        pltpu.make_async_copy(mixed, carried.at[block_at(me)], carry_recv_sem).start()
        pltpu.make_async_copy(carried, carried, carry_recv_sem).wait()
        out_ref[...] = carried[...]

    @pl.when((me < n - 1) & (me != half - 1))
    def _():
        pltpu.make_async_copy(carried, carried, carry_recv_sem).wait()
        for chunk in range(chunks):
            whole = ret.at[chunk]
            pltpu.make_async_copy(whole, whole, back_recv_sem.at[chunk]).wait()
            for block in range(col_blocks):
                at = pl.ds(block * block_cols + chunk * cols, cols)
                out_ref[:, at] = (
                    carried[:, at].astype(jnp.float32)
                    + ret[chunk, :, block * cols:(block + 1) * cols].astype(jnp.float32)
                ).astype(jnp.bfloat16)

    @pl.when(me == n - 1)
    def _():
        out_ref[...] = jnp.zeros_like(out_ref)

    @pl.when(carries)
    def _():
        carry().wait_send()

    @pl.when(me == half)
    def _():
        part = temporal.at[:, pl.ds(0, total - ROWS), :]
        pltpu.make_async_copy(part, part, middle_send_sem).wait()

    @pl.when(me != half - 1)
    def _():
        last.wait_send()

    ends = (me == n - 1) | (me == half - 1)

    for chunk in range(chunks):
        part = recv.at[chunk, :, pl.ds(0, total - ROWS), :]
        pltpu.make_async_copy(part, part, send_sem.at[chunk]).wait()

        @pl.when(jnp.logical_not(ends))
        def _():
            part = temporal.at[chunk, pl.ds(0, total - 3 * ROWS), :]
            pltpu.make_async_copy(part, part, back_send_sem.at[chunk]).wait()

        @pl.when(ends)
        def _():
            part = temporal.at[chunk, pl.ds(0, total - 2 * ROWS), :]
            pltpu.make_async_copy(part, part, back_send_sem.at[chunk]).wait()


def body(queries, key_rows, value_rows, slopes, noise_level, frame_times):
    n = lax.axis_size("frame")
    frame_rows, width = queries.shape
    head_count = slopes.shape[0]
    head_dim = width // head_count
    row_blocks = frame_rows // ROWS
    col_blocks = n // row_blocks
    block_cols = width // col_blocks
    chunks = math.gcd(block_cols // head_dim, 4)
    cols = block_cols // chunks
    total = n * ROWS
    plan = (frame_rows, width, head_count, head_dim, row_blocks, col_blocks, chunks)
    bf16, f32 = jnp.bfloat16, jnp.float32
    anywhere = pl.BlockSpec(memory_space=pltpu.HBM)
    return pl.pallas_call(
        functools.partial(kernel, n, plan),
        out_shape=jax.ShapeDtypeStruct((frame_rows, width), bf16),
        in_specs=[anywhere] * 6,
        out_specs=pl.BlockSpec(memory_space=pltpu.VMEM),
        scratch_shapes=[
            pltpu.VMEM((3, frame_rows, width), bf16),
            pltpu.VMEM((chunks, 3, total, cols), bf16),
            pltpu.VMEM((chunks, total, cols), bf16),
            pltpu.VMEM((chunks, frame_rows, col_blocks * cols), bf16),
            pltpu.VMEM((frame_rows, width), bf16),
            pltpu.VMEM((frame_rows, width), bf16),
            pltpu.VMEM((ROWS, block_cols), bf16),
            pltpu.VMEM((ROWS, block_cols), bf16),
            pltpu.VMEM((total, total), f32),
            pltpu.VMEM((n, LANES), f32),
            pltpu.VMEM((n, LANES), f32),
            pltpu.VMEM(slopes.shape, slopes.dtype),
            pltpu.SMEM(noise_level.shape, noise_level.dtype),
            pltpu.SMEM(frame_times.shape, frame_times.dtype),
            pltpu.VMEM((head_count, LANES), f32),
            pltpu.SemaphoreType.DMA((6,)),
            pltpu.SemaphoreType.DMA((chunks,)),
            pltpu.SemaphoreType.DMA((chunks,)),
            pltpu.SemaphoreType.DMA((chunks,)),
            pltpu.SemaphoreType.DMA((chunks,)),
            pltpu.SemaphoreType.DMA,
            pltpu.SemaphoreType.DMA,
            pltpu.SemaphoreType.DMA,
            pltpu.SemaphoreType.DMA,
            pltpu.SemaphoreType.DMA,
        ],
        compiler_params=pltpu.CompilerParams(
            collective_id=0, has_side_effects=True, vmem_limit_bytes=64 * 1024 * 1024
        ),
    )(slopes, noise_level, frame_times, queries, key_rows, value_rows)


def solution(mesh):
    return jax.shard_map(
        body,
        mesh=mesh,
        in_specs=(
            P(("groups", "frame"), None),
            P(("groups", "frame"), None),
            P(("groups", "frame"), None),
            P(),
            P("groups"),
            P("groups"),
        ),
        out_specs=P(("groups", "frame"), None),
        check_vma=False,
    )
```

```python
import functools
import math

import jax
import jax.numpy as jnp
from jax import lax
from jax.experimental import pallas as pl
from jax.experimental.pallas import tpu as pltpu
from jax.sharding import PartitionSpec as P

LEVELS = 1000
ROWS = 16
LANES = 128
FAR = 1e30
MESH = pl.DeviceIdType.MESH


def softmax_rows(scores):
    top = jnp.max(scores, axis=-1, keepdims=True)
    raised = jnp.exp(scores - top)
    return (raised * (1.0 / jnp.sum(raised, axis=-1, keepdims=True))).astype(jnp.bfloat16)


def scores_of(queries, keys):
    return lax.dot_general(
        queries, keys, (((1,), (1,)), ((), ())), preferred_element_type=jnp.float32
    )


def kernel(
    n, plan,
    slopes_hbm, level_hbm, times_hbm, q_ref, k_ref, v_ref, out_ref,
    qkv, recv, temporal, ret, sent, carried, middle, mixed, dist, signal_gate, noise_gate,
    slopes_ref, level_ref, times_ref, slope_rows,
    load_sem, send_sem, recv_sem, back_send_sem, back_recv_sem, carry_send_sem, carry_recv_sem,
    middle_send_sem, middle_recv_sem, mixed_send_sem, second, third, fourth,
):
    frame_rows, width, head_count, head_dim, row_blocks, col_blocks, chunks = plan
    block_cols = width // col_blocks
    cols = block_cols // chunks
    total = n * ROWS
    scale = 1.0 / math.sqrt(head_dim)
    half = n // 2
    me = lax.axis_index("frame")

    loads = [
        pltpu.make_async_copy(source, qkv.at[i], load_sem.at[i])
        for i, source in enumerate((q_ref, k_ref, v_ref))
    ]
    small = [
        pltpu.make_async_copy(source, target, load_sem.at[3 + i])
        for i, (source, target) in enumerate(
            ((slopes_hbm, slopes_ref), (level_hbm, level_ref), (times_hbm, times_ref))
        )
    ]
    barrier = pltpu.get_barrier_semaphore()

    part_size = n // 4
    quarter, place_in = lax.div(me, part_size), lax.rem(me, part_size)
    inner = (quarter == 1) | (quarter == 2)
    across = 3 - quarter
    outer = jnp.where(quarter == 1, 0, 3)
    beside = jnp.where(quarter == 0, 1, 2)

    def tell(semaphore, where, slot):
        pl.semaphore_signal(
            semaphore, inc=1, device_id={"frame": where * part_size + slot}, device_id_type=MESH
        )

    @pl.when(inner)
    def _():
        @pl.loop(0, part_size)
        def _(slot):
            tell(barrier, across, slot)

        @pl.loop(0, part_size)
        def _(slot):
            tell(barrier, outer, slot)

    for load in loads + small:
        load.start()
    pl.semaphore_wait(barrier, part_size)

    @pl.when(inner)
    def _():
        tell(second, across, place_in)

    @pl.when(jnp.logical_not(inner))
    def _():
        @pl.loop(0, part_size)
        def _(slot):
            tell(second, beside, slot)

    for load in loads:
        load.wait()

    def block_at(peer):
        row = pl.multiple_of(lax.div(peer, col_blocks) * ROWS, ROWS)
        col = pl.multiple_of(lax.rem(peer, col_blocks) * block_cols, LANES)
        return pl.ds(row, ROWS), pl.ds(col, block_cols)

    def piece(peer, chunk):
        row = pl.multiple_of(lax.div(peer, col_blocks) * ROWS, ROWS)
        col = pl.multiple_of(lax.rem(peer, col_blocks) * block_cols + chunk * cols, LANES)
        return qkv.at[:, pl.ds(row, ROWS), pl.ds(col, cols)]

    my_slot = pl.ds(pl.multiple_of(me * ROWS, ROWS), ROWS)
    my_rows = pl.ds(pl.multiple_of(lax.div(me, col_blocks) * ROWS, ROWS), ROWS)
    my_col = pl.ds(pl.multiple_of(lax.rem(me, col_blocks) * cols, LANES), cols)
    first_head = lax.rem(me, col_blocks) * (block_cols // head_dim)

    def send(peer, chunk):
        pltpu.make_async_remote_copy(
            src_ref=piece(peer, chunk),
            dst_ref=recv.at[chunk, :, my_slot, :],
            send_sem=send_sem.at[chunk],
            recv_sem=recv_sem.at[chunk],
            device_id={"frame": peer},
            device_id_type=MESH,
        ).start()

    @pl.when(inner)
    def _():
        @pl.loop(0, chunks)
        def _(chunk):
            @pl.loop(0, part_size)
            def _(step):
                send(across * part_size + lax.rem(place_in + step, part_size), chunk)

        pl.semaphore_wait(second, part_size + 1)
        tell(third, outer, place_in)
        tell(third, across, place_in)
        pl.semaphore_wait(third, 1)
        tell(fourth, outer, place_in)

    @pl.when(jnp.logical_not(inner))
    def _():
        pl.semaphore_wait(third, 1)
        pl.semaphore_wait(fourth, 1)

    @pl.loop(0, chunks)
    def _(chunk):
        @pl.loop(1, n)
        def _(step):
            peer = lax.rem(me + step, n)

            @pl.when(jnp.logical_not(inner & (lax.div(peer, part_size) == across)))
            def _():
                send(peer, chunk)

        pltpu.make_async_copy(
            piece(me, chunk), recv.at[chunk, :, my_slot, :], recv_sem.at[chunk]
        ).start()

    for load in small:
        load.wait()
    square = (head_count, head_count)
    diagonal = lax.broadcasted_iota(jnp.int32, square, 0) == lax.broadcasted_iota(jnp.int32, square, 1)
    spread = jnp.broadcast_to(slopes_ref[...].astype(jnp.float32).reshape(1, head_count), square)
    slope_rows[...] = jnp.broadcast_to(
        jnp.sum(jnp.where(diagonal, spread, 0.0), axis=1, keepdims=True), slope_rows.shape
    )

    row_frame = lax.broadcasted_iota(jnp.int32, (n, LANES), 0)

    def place(f, level):
        return jnp.where(row_frame == f, level_ref[f].astype(jnp.float32), level)

    level = lax.fori_loop(0, n, place, jnp.zeros((n, LANES), jnp.float32))
    phase = (level / LEVELS + 0.008) / 1.008
    cosine = jnp.cos(phase * (math.pi / 2))
    signal = cosine * cosine
    signal_gate[...] = jnp.sqrt(signal)
    noise_gate[...] = jnp.sqrt(1.0 - signal)

    own_gate = signal_gate[pl.ds(me, 1), :]

    @pl.loop(0, head_count, unroll=4)
    def _(h):
        at = pl.ds(pl.multiple_of(h * head_dim, LANES), head_dim)
        weights = softmax_rows(scores_of(qkv[0, :, at], qkv[1, :, at]) * scale)
        attended = jnp.dot(weights, qkv[2, :, at], preferred_element_type=jnp.float32)
        sent[:, at] = (attended * own_gate).astype(jnp.bfloat16)

    def carry():
        return pltpu.make_async_remote_copy(
            src_ref=sent,
            dst_ref=carried,
            send_sem=carry_send_sem,
            recv_sem=carry_recv_sem,
            device_id={"frame": lax.rem(me + n - 1, n)},
            device_id_type=MESH,
        )

    carries = (me > 0) & (me != half)

    @pl.when(carries)
    def _():
        carry().start()

    @pl.when(me == half)
    def _():
        @pl.loop(1, n)
        def _(step):
            peer = lax.rem(me + step, n)
            pltpu.make_async_remote_copy(
                src_ref=sent.at[block_at(peer)],
                dst_ref=middle,
                send_sem=middle_send_sem,
                recv_sem=middle_recv_sem,
                device_id={"frame": peer},
                device_id_type=MESH,
            ).start()

        pltpu.make_async_copy(sent.at[block_at(me)], middle, middle_recv_sem).start()

    column = lax.broadcasted_iota(jnp.int32, (ROWS, total), 1)
    token = lax.broadcasted_iota(jnp.int32, (ROWS, total), 0)
    same = lax.rem(column, ROWS) == token
    column_frame = lax.div(column, ROWS)

    def stamp(g, stamps):
        return jnp.where(column_frame == g, times_ref[g].astype(jnp.float32), stamps)

    stamps = lax.fori_loop(0, n, stamp, jnp.zeros((ROWS, total), jnp.float32))

    @pl.loop(0, n)
    def _(f):
        gap = jnp.abs(times_ref[f].astype(jnp.float32) - stamps)
        dist[pl.ds(pl.multiple_of(f * ROWS, ROWS), ROWS), :] = jnp.where(same, gap, FAR)

    group = math.gcd(n, 16)

    def temporal_block(chunk, head, start):
        at = pl.ds(head * head_dim, head_dim)
        rows = pl.ds(start * ROWS, group * ROWS) if isinstance(start, int) else pl.ds(
            pl.multiple_of(start * ROWS, ROWS), group * ROWS
        )
        slope = slope_rows[pl.ds(first_head + chunk * (cols // head_dim) + head, 1), :][:, :1]
        raw = scores_of(recv[chunk, 0, rows, at], recv[chunk, 1, :, at])
        weights = softmax_rows(raw * scale - slope * dist[rows, :])
        attended = jnp.dot(weights, recv[chunk, 2, :, at], preferred_element_type=jnp.float32)
        gates = noise_gate[pl.ds(start, group), :]
        gated = attended.reshape(group, ROWS, head_dim) * gates[:, None, :]
        temporal[chunk, rows, at] = gated.reshape(group * ROWS, head_dim).astype(jnp.bfloat16)

    for chunk in range(chunks):
        whole = recv.at[chunk]
        pltpu.make_async_copy(whole, whole, recv_sem.at[chunk]).wait()
        for head in range(cols // head_dim):
            if n == group:
                temporal_block(chunk, head, 0)
            else:
                @pl.loop(0, n // group)
                def _(i):
                    temporal_block(chunk, head, i * group)

        @pl.loop(0, n)
        def _(step):
            peer = lax.rem(me + step, n)

            @pl.when((peer < n - 1) & (peer != half - 1))
            def _():
                source = temporal.at[chunk, pl.ds(pl.multiple_of((peer + 1) * ROWS, ROWS), ROWS), :]
                target = ret.at[chunk, my_rows, my_col]

                @pl.when(step > 0)
                def _():
                    pltpu.make_async_remote_copy(
                        src_ref=source,
                        dst_ref=target,
                        send_sem=back_send_sem.at[chunk],
                        recv_sem=back_recv_sem.at[chunk],
                        device_id={"frame": peer},
                        device_id_type=MESH,
                    ).start()

                @pl.when(step == 0)
                def _():
                    pltpu.make_async_copy(source, target, back_recv_sem.at[chunk]).start()

    pltpu.make_async_copy(middle, middle, middle_recv_sem).wait()
    for chunk in range(chunks):
        at = pl.ds(chunk * cols, cols)
        mixed[:, at] = (
            temporal[chunk, half * ROWS:(half + 1) * ROWS, :].astype(jnp.float32)
            + middle[:, at].astype(jnp.float32)
        ).astype(jnp.bfloat16)
    last = pltpu.make_async_remote_copy(
        src_ref=mixed,
        dst_ref=carried.at[block_at(me)],
        send_sem=mixed_send_sem,
        recv_sem=carry_recv_sem,
        device_id={"frame": half - 1},
        device_id_type=MESH,
    )

    @pl.when(me != half - 1)
    def _():
        last.start()

    @pl.when(me == half - 1)
    def _():
        pltpu.make_async_copy(mixed, carried.at[block_at(me)], carry_recv_sem).start()
        pltpu.make_async_copy(carried, carried, carry_recv_sem).wait()
        out_ref[...] = carried[...]

    @pl.when((me < n - 1) & (me != half - 1))
    def _():
        pltpu.make_async_copy(carried, carried, carry_recv_sem).wait()
        for chunk in range(chunks):
            whole = ret.at[chunk]
            pltpu.make_async_copy(whole, whole, back_recv_sem.at[chunk]).wait()
            for block in range(col_blocks):
                at = pl.ds(block * block_cols + chunk * cols, cols)
                out_ref[:, at] = (
                    carried[:, at].astype(jnp.float32)
                    + ret[chunk, :, block * cols:(block + 1) * cols].astype(jnp.float32)
                ).astype(jnp.bfloat16)

    @pl.when(me == n - 1)
    def _():
        out_ref[...] = jnp.zeros_like(out_ref)

    @pl.when(carries)
    def _():
        carry().wait_send()

    @pl.when(me == half)
    def _():
        part = temporal.at[:, pl.ds(0, total - ROWS), :]
        pltpu.make_async_copy(part, part, middle_send_sem).wait()

    @pl.when(me != half - 1)
    def _():
        last.wait_send()

    ends = (me == n - 1) | (me == half - 1)

    for chunk in range(chunks):
        part = recv.at[chunk, :, pl.ds(0, total - ROWS), :]
        pltpu.make_async_copy(part, part, send_sem.at[chunk]).wait()

        @pl.when(jnp.logical_not(ends))
        def _():
            part = temporal.at[chunk, pl.ds(0, total - 3 * ROWS), :]
            pltpu.make_async_copy(part, part, back_send_sem.at[chunk]).wait()

        @pl.when(ends)
        def _():
            part = temporal.at[chunk, pl.ds(0, total - 2 * ROWS), :]
            pltpu.make_async_copy(part, part, back_send_sem.at[chunk]).wait()


def body(queries, key_rows, value_rows, slopes, noise_level, frame_times):
    n = lax.axis_size("frame")
    frame_rows, width = queries.shape
    head_count = slopes.shape[0]
    head_dim = width // head_count
    row_blocks = frame_rows // ROWS
    col_blocks = n // row_blocks
    block_cols = width // col_blocks
    chunks = math.gcd(block_cols // head_dim, 2)
    cols = block_cols // chunks
    total = n * ROWS
    plan = (frame_rows, width, head_count, head_dim, row_blocks, col_blocks, chunks)
    bf16, f32 = jnp.bfloat16, jnp.float32
    anywhere = pl.BlockSpec(memory_space=pltpu.HBM)
    return pl.pallas_call(
        functools.partial(kernel, n, plan),
        out_shape=jax.ShapeDtypeStruct((frame_rows, width), bf16),
        in_specs=[anywhere] * 6,
        out_specs=pl.BlockSpec(memory_space=pltpu.VMEM),
        scratch_shapes=[
            pltpu.VMEM((3, frame_rows, width), bf16),
            pltpu.VMEM((chunks, 3, total, cols), bf16),
            pltpu.VMEM((chunks, total, cols), bf16),
            pltpu.VMEM((chunks, frame_rows, col_blocks * cols), bf16),
            pltpu.VMEM((frame_rows, width), bf16),
            pltpu.VMEM((frame_rows, width), bf16),
            pltpu.VMEM((ROWS, block_cols), bf16),
            pltpu.VMEM((ROWS, block_cols), bf16),
            pltpu.VMEM((total, total), f32),
            pltpu.VMEM((n, LANES), f32),
            pltpu.VMEM((n, LANES), f32),
            pltpu.VMEM(slopes.shape, slopes.dtype),
            pltpu.SMEM(noise_level.shape, noise_level.dtype),
            pltpu.SMEM(frame_times.shape, frame_times.dtype),
            pltpu.VMEM((head_count, LANES), f32),
            pltpu.SemaphoreType.DMA((6,)),
            pltpu.SemaphoreType.DMA((chunks,)),
            pltpu.SemaphoreType.DMA((chunks,)),
            pltpu.SemaphoreType.DMA((chunks,)),
            pltpu.SemaphoreType.DMA((chunks,)),
            pltpu.SemaphoreType.DMA,
            pltpu.SemaphoreType.DMA,
            pltpu.SemaphoreType.DMA,
            pltpu.SemaphoreType.DMA,
            pltpu.SemaphoreType.DMA,
            pltpu.SemaphoreType.REGULAR,
            pltpu.SemaphoreType.REGULAR,
            pltpu.SemaphoreType.REGULAR,
        ],
        compiler_params=pltpu.CompilerParams(
            collective_id=0, has_side_effects=True, vmem_limit_bytes=64 * 1024 * 1024
        ),
    )(slopes, noise_level, frame_times, queries, key_rows, value_rows)


def solution(mesh):
    return jax.shard_map(
        body,
        mesh=mesh,
        in_specs=(
            P(("groups", "frame"), None),
            P(("groups", "frame"), None),
            P(("groups", "frame"), None),
            P(),
            P("groups"),
            P("groups"),
        ),
        out_specs=P(("groups", "frame"), None),
        check_vma=False,
    )
```

```python
import functools
import math

import jax
import jax.numpy as jnp
from jax import lax
from jax.experimental import pallas as pl
from jax.experimental.pallas import tpu as pltpu
from jax.sharding import PartitionSpec as P

LEVELS = 1000
ROWS = 16
LANES = 128
FAR = 1e30
MESH = pl.DeviceIdType.MESH


def softmax_rows(scores):
    top = jnp.max(scores, axis=-1, keepdims=True)
    raised = jnp.exp(scores - top)
    return (raised * (1.0 / jnp.sum(raised, axis=-1, keepdims=True))).astype(jnp.bfloat16)


def scores_of(queries, keys):
    return lax.dot_general(
        queries, keys, (((1,), (1,)), ((), ())), preferred_element_type=jnp.float32
    )


def kernel(
    n, plan,
    slopes_hbm, level_hbm, times_hbm, q_ref, k_ref, v_ref, out_ref,
    qkv, recv, temporal, ret, sent, carried, middle, mixed, dist, signal_gate, noise_gate,
    slopes_ref, level_ref, times_ref, slope_rows,
    load_sem, send_sem, recv_sem, back_send_sem, back_recv_sem, carry_send_sem, carry_recv_sem,
    middle_send_sem, middle_recv_sem, mixed_send_sem, second, third, fourth,
    relay, relay_send_sem, relay_recv_sem, relay_out_sem,
):
    frame_rows, width, head_count, head_dim, row_blocks, col_blocks, chunks = plan
    block_cols = width // col_blocks
    cols = block_cols // chunks
    total = n * ROWS
    scale = 1.0 / math.sqrt(head_dim)
    half = n // 2
    me = lax.axis_index("frame")

    loads = [
        pltpu.make_async_copy(source, qkv.at[i], load_sem.at[i])
        for i, source in enumerate((q_ref, k_ref, v_ref))
    ]
    small = [
        pltpu.make_async_copy(source, target, load_sem.at[3 + i])
        for i, (source, target) in enumerate(
            ((slopes_hbm, slopes_ref), (level_hbm, level_ref), (times_hbm, times_ref))
        )
    ]
    barrier = pltpu.get_barrier_semaphore()

    part_size = n // 4
    quarter, place_in = lax.div(me, part_size), lax.rem(me, part_size)
    inner = (quarter == 1) | (quarter == 2)
    across = 3 - quarter
    outer = jnp.where(quarter == 1, 0, 3)
    beside = jnp.where(quarter == 0, 1, 2)

    def tell(semaphore, where, slot):
        pl.semaphore_signal(
            semaphore, inc=1, device_id={"frame": where * part_size + slot}, device_id_type=MESH
        )

    @pl.when(inner)
    def _():
        @pl.loop(0, part_size)
        def _(slot):
            tell(barrier, across, slot)

        @pl.loop(0, part_size)
        def _(slot):
            tell(barrier, outer, slot)

    for load in loads + small:
        load.start()
    pl.semaphore_wait(barrier, part_size)

    @pl.when(inner)
    def _():
        tell(second, across, place_in)

    @pl.when(jnp.logical_not(inner))
    def _():
        @pl.loop(0, part_size)
        def _(slot):
            tell(second, beside, slot)

    for load in loads:
        load.wait()

    def block_at(peer):
        row = pl.multiple_of(lax.div(peer, col_blocks) * ROWS, ROWS)
        col = pl.multiple_of(lax.rem(peer, col_blocks) * block_cols, LANES)
        return pl.ds(row, ROWS), pl.ds(col, block_cols)

    def piece(peer, chunk):
        row = pl.multiple_of(lax.div(peer, col_blocks) * ROWS, ROWS)
        col = pl.multiple_of(lax.rem(peer, col_blocks) * block_cols + chunk * cols, LANES)
        return qkv.at[:, pl.ds(row, ROWS), pl.ds(col, cols)]

    my_slot = pl.ds(pl.multiple_of(me * ROWS, ROWS), ROWS)
    my_rows = pl.ds(pl.multiple_of(lax.div(me, col_blocks) * ROWS, ROWS), ROWS)
    my_col = pl.ds(pl.multiple_of(lax.rem(me, col_blocks) * cols, LANES), cols)
    first_head = lax.rem(me, col_blocks) * (block_cols // head_dim)

    def send(peer, chunk):
        pltpu.make_async_remote_copy(
            src_ref=piece(peer, chunk),
            dst_ref=recv.at[chunk, :, my_slot, :],
            send_sem=send_sem.at[chunk],
            recv_sem=recv_sem.at[chunk],
            device_id={"frame": peer},
            device_id_type=MESH,
        ).start()

    @pl.when(inner)
    def _():
        @pl.loop(0, chunks)
        def _(chunk):
            @pl.loop(0, part_size)
            def _(step):
                send(across * part_size + lax.rem(place_in + step, part_size), chunk)

        pl.semaphore_wait(second, part_size + 1)
        tell(third, outer, place_in)
        tell(third, across, place_in)
        pl.semaphore_wait(third, 1)
        tell(fourth, outer, place_in)

    @pl.when(jnp.logical_not(inner))
    def _():
        pl.semaphore_wait(third, 1)
        pl.semaphore_wait(fourth, 1)

    @pl.loop(0, chunks)
    def _(chunk):
        @pl.loop(1, n)
        def _(step):
            peer = lax.rem(me + step, n)

            @pl.when(jnp.logical_not(inner & (lax.div(peer, part_size) == across)))
            def _():
                send(peer, chunk)

        pltpu.make_async_copy(
            piece(me, chunk), recv.at[chunk, :, my_slot, :], recv_sem.at[chunk]
        ).start()

    for load in small:
        load.wait()
    square = (head_count, head_count)
    diagonal = lax.broadcasted_iota(jnp.int32, square, 0) == lax.broadcasted_iota(jnp.int32, square, 1)
    spread = jnp.broadcast_to(slopes_ref[...].astype(jnp.float32).reshape(1, head_count), square)
    slope_rows[...] = jnp.broadcast_to(
        jnp.sum(jnp.where(diagonal, spread, 0.0), axis=1, keepdims=True), slope_rows.shape
    )

    row_frame = lax.broadcasted_iota(jnp.int32, (n, LANES), 0)

    def place(f, level):
        return jnp.where(row_frame == f, level_ref[f].astype(jnp.float32), level)

    level = lax.fori_loop(0, n, place, jnp.zeros((n, LANES), jnp.float32))
    phase = (level / LEVELS + 0.008) / 1.008
    cosine = jnp.cos(phase * (math.pi / 2))
    signal = cosine * cosine
    signal_gate[...] = jnp.sqrt(signal)
    noise_gate[...] = jnp.sqrt(1.0 - signal)

    own_gate = signal_gate[pl.ds(me, 1), :]

    @pl.loop(0, head_count, unroll=4)
    def _(h):
        at = pl.ds(pl.multiple_of(h * head_dim, LANES), head_dim)
        weights = softmax_rows(scores_of(qkv[0, :, at], qkv[1, :, at]) * scale)
        attended = jnp.dot(weights, qkv[2, :, at], preferred_element_type=jnp.float32)
        sent[:, at] = (attended * own_gate).astype(jnp.bfloat16)

    def carry():
        return pltpu.make_async_remote_copy(
            src_ref=sent,
            dst_ref=carried,
            send_sem=carry_send_sem,
            recv_sem=carry_recv_sem,
            device_id={"frame": lax.rem(me + n - 1, n)},
            device_id_type=MESH,
        )

    carries = (me > 0) & (me != half)
    relay_device = half + part_size // 2
    handed = pltpu.make_async_remote_copy(
        src_ref=sent.at[pl.ds(frame_rows // 4, frame_rows // 4), :],
        dst_ref=relay,
        send_sem=relay_send_sem,
        recv_sem=relay_recv_sem,
        device_id={"frame": relay_device},
        device_id_type=MESH,
    )

    @pl.when(carries)
    def _():
        carry().start()

    @pl.when(me == half)
    def _():
        @pl.loop(1, n)
        def _(step):
            peer = lax.rem(me + step, n)

            @pl.when((peer < half // 2) | (peer >= half))
            def _():
                pltpu.make_async_remote_copy(
                    src_ref=sent.at[block_at(peer)],
                    dst_ref=middle,
                    send_sem=middle_send_sem,
                    recv_sem=middle_recv_sem,
                    device_id={"frame": peer},
                    device_id_type=MESH,
                ).start()

        pltpu.make_async_copy(sent.at[block_at(me)], middle, middle_recv_sem).start()
        handed.start()

    column = lax.broadcasted_iota(jnp.int32, (ROWS, total), 1)
    token = lax.broadcasted_iota(jnp.int32, (ROWS, total), 0)
    same = lax.rem(column, ROWS) == token
    column_frame = lax.div(column, ROWS)

    def stamp(g, stamps):
        return jnp.where(column_frame == g, times_ref[g].astype(jnp.float32), stamps)

    stamps = lax.fori_loop(0, n, stamp, jnp.zeros((ROWS, total), jnp.float32))

    @pl.loop(0, n)
    def _(f):
        gap = jnp.abs(times_ref[f].astype(jnp.float32) - stamps)
        dist[pl.ds(pl.multiple_of(f * ROWS, ROWS), ROWS), :] = jnp.where(same, gap, FAR)

    group = math.gcd(n, 16)

    def temporal_block(chunk, head, start):
        at = pl.ds(head * head_dim, head_dim)
        rows = pl.ds(start * ROWS, group * ROWS) if isinstance(start, int) else pl.ds(
            pl.multiple_of(start * ROWS, ROWS), group * ROWS
        )
        slope = slope_rows[pl.ds(first_head + chunk * (cols // head_dim) + head, 1), :][:, :1]
        raw = scores_of(recv[chunk, 0, rows, at], recv[chunk, 1, :, at])
        weights = softmax_rows(raw * scale - slope * dist[rows, :])
        attended = jnp.dot(weights, recv[chunk, 2, :, at], preferred_element_type=jnp.float32)
        gates = noise_gate[pl.ds(start, group), :]
        gated = attended.reshape(group, ROWS, head_dim) * gates[:, None, :]
        temporal[chunk, rows, at] = gated.reshape(group * ROWS, head_dim).astype(jnp.bfloat16)

    for chunk in range(chunks):
        if chunk == chunks - 1:
            @pl.when(me == relay_device)
            def _():
                handed.wait_recv()

                @pl.loop(half // 2, half)
                def _(peer):
                    row = pl.multiple_of(
                        lax.div(peer, col_blocks) * ROWS - frame_rows // 4, ROWS
                    )
                    pltpu.make_async_remote_copy(
                        src_ref=relay.at[pl.ds(row, ROWS), block_at(peer)[1]],
                        dst_ref=middle,
                        send_sem=relay_out_sem,
                        recv_sem=middle_recv_sem,
                        device_id={"frame": peer},
                        device_id_type=MESH,
                    ).start()

        whole = recv.at[chunk]
        pltpu.make_async_copy(whole, whole, recv_sem.at[chunk]).wait()
        for head in range(cols // head_dim):
            if n == group:
                temporal_block(chunk, head, 0)
            else:
                @pl.loop(0, n // group)
                def _(i):
                    temporal_block(chunk, head, i * group)

        @pl.loop(0, n)
        def _(step):
            peer = lax.rem(me + step, n)

            @pl.when((peer < n - 1) & (peer != half - 1))
            def _():
                source = temporal.at[chunk, pl.ds(pl.multiple_of((peer + 1) * ROWS, ROWS), ROWS), :]
                target = ret.at[chunk, my_rows, my_col]

                @pl.when(step > 0)
                def _():
                    pltpu.make_async_remote_copy(
                        src_ref=source,
                        dst_ref=target,
                        send_sem=back_send_sem.at[chunk],
                        recv_sem=back_recv_sem.at[chunk],
                        device_id={"frame": peer},
                        device_id_type=MESH,
                    ).start()

                @pl.when(step == 0)
                def _():
                    pltpu.make_async_copy(source, target, back_recv_sem.at[chunk]).start()

    pltpu.make_async_copy(middle, middle, middle_recv_sem).wait()
    for chunk in range(chunks):
        at = pl.ds(chunk * cols, cols)
        mixed[:, at] = (
            temporal[chunk, half * ROWS:(half + 1) * ROWS, :].astype(jnp.float32)
            + middle[:, at].astype(jnp.float32)
        ).astype(jnp.bfloat16)
    last = pltpu.make_async_remote_copy(
        src_ref=mixed,
        dst_ref=carried.at[block_at(me)],
        send_sem=mixed_send_sem,
        recv_sem=carry_recv_sem,
        device_id={"frame": half - 1},
        device_id_type=MESH,
    )

    @pl.when(me != half - 1)
    def _():
        last.start()

    @pl.when(me == half - 1)
    def _():
        pltpu.make_async_copy(mixed, carried.at[block_at(me)], carry_recv_sem).start()
        pltpu.make_async_copy(carried, carried, carry_recv_sem).wait()
        out_ref[...] = carried[...]

    @pl.when((me < n - 1) & (me != half - 1))
    def _():
        pltpu.make_async_copy(carried, carried, carry_recv_sem).wait()
        for chunk in range(chunks):
            whole = ret.at[chunk]
            pltpu.make_async_copy(whole, whole, back_recv_sem.at[chunk]).wait()
            for block in range(col_blocks):
                at = pl.ds(block * block_cols + chunk * cols, cols)
                out_ref[:, at] = (
                    carried[:, at].astype(jnp.float32)
                    + ret[chunk, :, block * cols:(block + 1) * cols].astype(jnp.float32)
                ).astype(jnp.bfloat16)

    @pl.when(me == n - 1)
    def _():
        out_ref[...] = jnp.zeros_like(out_ref)

    @pl.when(carries)
    def _():
        carry().wait_send()

    @pl.when(me == half)
    def _():
        part = temporal.at[:, pl.ds(0, total - (1 + half // 2) * ROWS), :]
        pltpu.make_async_copy(part, part, middle_send_sem).wait()
        handed.wait_send()

    @pl.when(me == relay_device)
    def _():
        part = temporal.at[:, pl.ds(0, half // 2 * ROWS), :]
        pltpu.make_async_copy(part, part, relay_out_sem).wait()

    @pl.when(me != half - 1)
    def _():
        last.wait_send()

    ends = (me == n - 1) | (me == half - 1)

    for chunk in range(chunks):
        part = recv.at[chunk, :, pl.ds(0, total - ROWS), :]
        pltpu.make_async_copy(part, part, send_sem.at[chunk]).wait()

        @pl.when(jnp.logical_not(ends))
        def _():
            part = temporal.at[chunk, pl.ds(0, total - 3 * ROWS), :]
            pltpu.make_async_copy(part, part, back_send_sem.at[chunk]).wait()

        @pl.when(ends)
        def _():
            part = temporal.at[chunk, pl.ds(0, total - 2 * ROWS), :]
            pltpu.make_async_copy(part, part, back_send_sem.at[chunk]).wait()


def body(queries, key_rows, value_rows, slopes, noise_level, frame_times):
    n = lax.axis_size("frame")
    frame_rows, width = queries.shape
    head_count = slopes.shape[0]
    head_dim = width // head_count
    row_blocks = frame_rows // ROWS
    col_blocks = n // row_blocks
    block_cols = width // col_blocks
    chunks = math.gcd(block_cols // head_dim, 2)
    cols = block_cols // chunks
    total = n * ROWS
    plan = (frame_rows, width, head_count, head_dim, row_blocks, col_blocks, chunks)
    bf16, f32 = jnp.bfloat16, jnp.float32
    anywhere = pl.BlockSpec(memory_space=pltpu.HBM)
    return pl.pallas_call(
        functools.partial(kernel, n, plan),
        out_shape=jax.ShapeDtypeStruct((frame_rows, width), bf16),
        in_specs=[anywhere] * 6,
        out_specs=pl.BlockSpec(memory_space=pltpu.VMEM),
        scratch_shapes=[
            pltpu.VMEM((3, frame_rows, width), bf16),
            pltpu.VMEM((chunks, 3, total, cols), bf16),
            pltpu.VMEM((chunks, total, cols), bf16),
            pltpu.VMEM((chunks, frame_rows, col_blocks * cols), bf16),
            pltpu.VMEM((frame_rows, width), bf16),
            pltpu.VMEM((frame_rows, width), bf16),
            pltpu.VMEM((ROWS, block_cols), bf16),
            pltpu.VMEM((ROWS, block_cols), bf16),
            pltpu.VMEM((total, total), f32),
            pltpu.VMEM((n, LANES), f32),
            pltpu.VMEM((n, LANES), f32),
            pltpu.VMEM(slopes.shape, slopes.dtype),
            pltpu.SMEM(noise_level.shape, noise_level.dtype),
            pltpu.SMEM(frame_times.shape, frame_times.dtype),
            pltpu.VMEM((head_count, LANES), f32),
            pltpu.SemaphoreType.DMA((6,)),
            pltpu.SemaphoreType.DMA((chunks,)),
            pltpu.SemaphoreType.DMA((chunks,)),
            pltpu.SemaphoreType.DMA((chunks,)),
            pltpu.SemaphoreType.DMA((chunks,)),
            pltpu.SemaphoreType.DMA,
            pltpu.SemaphoreType.DMA,
            pltpu.SemaphoreType.DMA,
            pltpu.SemaphoreType.DMA,
            pltpu.SemaphoreType.DMA,
            pltpu.SemaphoreType.REGULAR,
            pltpu.SemaphoreType.REGULAR,
            pltpu.SemaphoreType.REGULAR,
            pltpu.VMEM((frame_rows // 4, width), bf16),
            pltpu.SemaphoreType.DMA,
            pltpu.SemaphoreType.DMA,
            pltpu.SemaphoreType.DMA,
        ],
        compiler_params=pltpu.CompilerParams(
            collective_id=0, has_side_effects=True, vmem_limit_bytes=64 * 1024 * 1024
        ),
    )(slopes, noise_level, frame_times, queries, key_rows, value_rows)


def solution(mesh):
    return jax.shard_map(
        body,
        mesh=mesh,
        in_specs=(
            P(("groups", "frame"), None),
            P(("groups", "frame"), None),
            P(("groups", "frame"), None),
            P(),
            P("groups"),
            P("groups"),
        ),
        out_specs=P(("groups", "frame"), None),
        check_vma=False,
    )
```
